32 devices in a mesh: groups: 2 (over x), wide: 16 (over z, y, core).
Axes of the slice: x: 2, y: 2, z: 4, core: 2. Of those that a mesh axis runs over, the one named last changes fastest.
Arguments:
- residual: bfloat16 [128, 8192], P(('groups', 'wide')), parts along dimension 0
- norm_gain: float32 [8192], replicated, may hold values from 0.1 to 1.9
- query_weight: bfloat16 [8192, 8192], P(None, 'wide'), may hold values from -0.0625 to 0.0625
- key_weight: bfloat16 [8192, 1024], P(None, 'wide'), may hold values from -0.0625 to 0.0625
- value_weight: bfloat16 [8192, 1024], P(None, 'wide'), may hold values from -0.0625 to 0.0625
- output_weight: bfloat16 [8192, 8192], P(None, 'wide'), may hold values from -0.0625 to 0.0625
- past_cache: bfloat16 [128, 2, 8, 512, 128], P(('groups', 'wide')), parts along dimension 0, as said below
- lengths: int32 [128], P(('groups', 'wide')), parts along dimension 0, may hold values from 1 to 512, 16384 in all
Outputs:
- final_state: bfloat16 [128, 8192], P(('groups', 'wide')), parts along dimension 0
- new_entries: bfloat16 [128, 2, 2048], P(('groups', 'wide')), parts along dimension 0
The draws below stay inside these ranges and needn't reach their ends.
There are 2 independent parts, one for each index of `groups`. The reference program is written for one: setup_inputs(seed, part) draws one part's arguments, and reference() takes and returns one part's arrays. A program takes and returns all parts, laid end to end along the dimension named above; an argument that names none is the same for every part. Nothing has to cross between parts.
Inputs may be any that keep to these rules, and one draw needn't show every extreme that they name: past_cache[r, 0] holds robot r's cached keys, already rotated to their positions; past_cache[r, 1] its values. lengths[r] slots of robot r's 512 are filled, from slot 0 on; some robot fills all.
All inputs are finite; a program needn't handle non-finite values. No bound on the sum of `lengths` on one device may be relied on, other than what follows from the above.
Results may differ from the reference program's by a relative error of at most 0.02.
The reference program's roundings to bfloat16 on the way count: a program that leaves them out, or rounds other values in their place, can miss the bound.
Values may be sent and summed in bfloat16 or wider, within the bound.
A program may use at most 128 MiB of HBM per device.

```python
import math
from functools import partial
import jax
import jax.numpy as jnp
import numpy as np
from jax import lax

D = 8192
QH = 64
KVH = 8
HD = 128
CTX = 512
STEPS = 2
ROBOTS = 64


def draw_residual(key, part):
    key = jax.random.fold_in(key, 11)
    key_rows, key_cells = jax.random.split(key)
    column = jnp.arange(D, dtype=jnp.float32) / max(D - 1, 1)
    row_scale = jnp.exp(jax.random.uniform(key_rows, (ROBOTS, 1), jnp.float32, math.log(0.3), math.log(3.0)))
    base_draw = jax.random.normal(key_cells, (ROBOTS, D), jnp.float32)
    column_scale = 0.1 * 10.0 ** column
    return (base_draw * row_scale * column_scale[None, :]).astype(jnp.bfloat16)


def draw_past_cache(key, part):
    key = jax.random.fold_in(key, 23)
    key_keys, key_values = jax.random.split(key, 2)
    shape = (ROBOTS, KVH, CTX, HD)
    past_keys = jax.random.normal(key_keys, shape, jnp.float32)
    past_values = jax.random.normal(key_values, shape, jnp.float32)
    return jnp.stack([past_keys, past_values], axis=1).astype(jnp.bfloat16)


def shard_levels(stream_key, dims, shards, smallest, high):
    level = 1.0
    for position, parts in shards:
        draws = jax.random.uniform(jax.random.fold_in(jax.random.fold_in(stream_key, 6), position), (parts,), jnp.float32, smallest / len(shards), high / len(shards))
        level = level * jnp.repeat(jnp.exp(draws), dims[position] // parts).reshape((-1,) + (1,) * (len(dims) - 1 - position))
    return level


def length_profile(amount, total, bound, skew):
    loads = [(1 << 20) // math.isqrt(grade ** skew) + 1 for grade in range(2, amount + 1)]
    rest, holding = total - bound - (amount - 1), [1] * (amount - 1)
    while rest > 0:
        candidates = [i for i in range(amount - 1) if holding[i] < bound]
        mass, budget = sum([loads[i] for i in candidates]), rest
        for i in candidates:
            addition = min(bound - holding[i], max(1, budget * loads[i] // mass), rest)
            holding[i] = holding[i] + addition
            rest = rest - addition
    return np.array([bound] + holding)


def ragged(key, amount, total, most, lean):
    if amount == 2:
        one = jax.random.randint(key, (), max(1, total - most), min(most, total - 1) + 1)
        return jnp.stack([one, total - one])
    sizes = jnp.asarray(length_profile(amount, total, most, lean), jnp.int32)
    couples = (amount - 1) // 2
    giver, sink = sizes[1:1 + 2 * couples:2], sizes[2:2 + 2 * couples:2]
    slack = jnp.minimum(giver - 1, most - sink)
    passed = jax.random.randint(jax.random.fold_in(key, 1), (couples,), 0, 1 << 20) % (slack + 1)
    sizes = sizes.at[1:1 + 2 * couples:2].set(giver - passed).at[2:2 + 2 * couples:2].set(sink + passed)
    return sizes[jax.random.permutation(jax.random.fold_in(key, 2), amount)]


def gaussian(own_key, dims, deviation, most, pieces=(), kind=jnp.bfloat16):
    values = jax.random.normal(own_key, dims, jnp.float32) * deviation
    if len(pieces) > 0:
        values = shard_levels(own_key, dims, pieces, -0.22, 0.18) * values
    return jnp.clip(values, min=-most, max=most).astype(kind)


def setup_inputs(seed: int = 0, part: int = 0) -> dict:
    streams_of = jax.random.split(jax.random.key(seed), 9)
    own_keys = jax.random.split(jax.random.fold_in(streams_of[8], part), 9)
    return {
        "residual": draw_residual(jax.random.fold_in(jax.random.fold_in(streams_of[8], part), 71), part),
        "norm_gain": jnp.clip(1.0 + 0.18 * jax.random.normal(streams_of[1], (D,), jnp.float32), 0.1, 1.9),
        "query_weight": gaussian(streams_of[2], (D, QH * HD), D ** -0.5, 0.0625, ((1, 16),)),
        "key_weight": gaussian(streams_of[3], (D, KVH * HD), D ** -0.5, 0.0625, ((1, 16),)),
        "value_weight": gaussian(streams_of[4], (D, KVH * HD), D ** -0.5, 0.0625, ((1, 16),)),
        "output_weight": gaussian(streams_of[5], (QH * HD, D), (QH * HD) ** -0.5, 0.0625, ((1, 16),)),
        "past_cache": draw_past_cache(jax.random.fold_in(jax.random.fold_in(streams_of[8], part), 71), part),
        "lengths": ragged(own_keys[7], ROBOTS, ROBOTS * CTX // 2, CTX, 0).astype(jnp.int32),
    }


rope_base = 500000.0
norm_eps = 1e-05

def rotate_heads(heads_block, positions):
    head_size = heads_block.shape[-1]
    half_size = head_size // 2
    frequency = rope_base ** (-2.0 * jnp.arange(half_size, dtype=jnp.float32) / head_size)
    angles = positions.astype(jnp.float32)[:, None, None] * frequency[None, None, :]
    cosine = jnp.cos(angles)
    sine_part = jnp.sin(angles)
    values = lax.optimization_barrier(heads_block).astype(jnp.float32)
    first_half = values[..., :half_size]
    second = values[..., half_size:]
    return jnp.concatenate([first_half * cosine - second * sine_part, second * cosine + first_half * sine_part], axis=-1).astype(jnp.bfloat16)

def attend_one(items, step_now):
    queries, cache_block, fresh_keys, fresh_values, length = lax.optimization_barrier(items)
    kv_heads = cache_block.shape[1]
    head_count, head_size = queries.shape
    grouped = queries.reshape(kv_heads, head_count // kv_heads, head_size).astype(jnp.float32)
    score_scale = 1.0 / math.sqrt(head_size)
    past_scores = jnp.einsum('kgd,kcd->kgc', grouped, cache_block[0].astype(jnp.float32)) * score_scale
    fresh_scores = jnp.einsum('kgd,skd->kgs', grouped, fresh_keys.astype(jnp.float32)) * score_scale
    slot_index = jnp.arange(cache_block.shape[2], dtype=jnp.int32)
    past_scores = jnp.where(slot_index[None, None, :] < length, past_scores, -jnp.inf)
    turn_index = jnp.arange(fresh_keys.shape[0], dtype=jnp.int32)
    fresh_scores = jnp.where(turn_index[None, None, :] <= step_now, fresh_scores, -jnp.inf)
    peak_score = jnp.maximum(lax.optimization_barrier(jnp.max(past_scores, axis=-1)), lax.optimization_barrier(jnp.max(fresh_scores, axis=-1)))
    past_exp = jnp.exp(past_scores - peak_score[..., None])
    fresh_exp = jnp.exp(fresh_scores - peak_score[..., None])
    denominator = lax.optimization_barrier(jnp.sum(past_exp, axis=-1)) + lax.optimization_barrier(jnp.sum(fresh_exp, axis=-1))
    past_weights = lax.optimization_barrier((past_exp / denominator[..., None]).astype(jnp.bfloat16)).astype(jnp.float32)
    fresh_weights = lax.optimization_barrier((fresh_exp / denominator[..., None]).astype(jnp.bfloat16)).astype(jnp.float32)
    context = jnp.einsum('kgc,kcd->kgd', past_weights, cache_block[1].astype(jnp.float32))
    context = context + jnp.einsum('kgs,skd->kgd', fresh_weights, fresh_values.astype(jnp.float32))
    return context.reshape(head_count * head_size).astype(jnp.bfloat16)

def reference(residual, norm_gain, query_weight, key_weight, value_weight, output_weight, past_cache, lengths):
    stream = residual
    fresh_keys = jnp.zeros((ROBOTS, STEPS, KVH, HD), jnp.bfloat16)
    fresh_values = jnp.zeros((ROBOTS, STEPS, KVH, HD), jnp.bfloat16)
    for step_now in range(STEPS):
        widened = lax.optimization_barrier(stream).astype(jnp.float32)
        inverse_rms = lax.rsqrt(lax.optimization_barrier(jnp.sum(widened * widened, axis=1)) / D + norm_eps)
        normed = (widened * inverse_rms[:, None] * norm_gain[None, :]).astype(jnp.bfloat16)
        queries = jnp.dot(normed, query_weight, preferred_element_type=jnp.float32).astype(jnp.bfloat16)
        new_keys = jnp.dot(normed, key_weight, preferred_element_type=jnp.float32).astype(jnp.bfloat16)
        new_values = jnp.dot(normed, value_weight, preferred_element_type=jnp.float32).astype(jnp.bfloat16)
        positions = lengths + step_now
        queries = rotate_heads(queries.reshape(ROBOTS, QH, HD), positions)
        new_keys = rotate_heads(new_keys.reshape(ROBOTS, KVH, HD), positions)
        fresh_keys = fresh_keys.at[:, step_now].set(new_keys)
        fresh_values = fresh_values.at[:, step_now].set(new_values.reshape(ROBOTS, KVH, HD))
        context = lax.map(partial(attend_one, step_now=step_now), (queries, past_cache, fresh_keys, fresh_values, lengths))
        attended = jnp.dot(context, output_weight, preferred_element_type=jnp.float32).astype(jnp.bfloat16)
        stream = (lax.optimization_barrier(stream).astype(jnp.float32) + lax.optimization_barrier(attended).astype(jnp.float32)).astype(jnp.bfloat16)
    new_entries = jnp.concatenate([fresh_keys.reshape(ROBOTS, STEPS, KVH * HD), fresh_values.reshape(ROBOTS, STEPS, KVH * HD)], axis=2)
    return (stream, new_entries)
```

```python
import math
from functools import partial

import jax
import jax.numpy as jnp
from jax import lax
from jax.experimental import pallas as pl
from jax.experimental.pallas import tpu as pltpu
from jax.sharding import PartitionSpec as P

QH = 64
KVH = 8
HD = 128
STEPS = 2


rope_base = 500000.0
norm_eps = 1e-05


def rotate_heads(heads_block, positions):
    head_size = heads_block.shape[-1]
    half_size = head_size // 2
    frequency = rope_base ** (-2.0 * jnp.arange(half_size, dtype=jnp.float32) / head_size)
    angles = positions.astype(jnp.float32)[:, None, None] * frequency[None, None, :]
    cosine = jnp.cos(angles)
    sine_part = jnp.sin(angles)
    values = heads_block.astype(jnp.float32)
    first_half = values[..., :half_size]
    second = values[..., half_size:]
    return jnp.concatenate(
        [first_half * cosine - second * sine_part, second * cosine + first_half * sine_part],
        axis=-1,
    ).astype(jnp.bfloat16)


def attend_local(queries, past_cache, fresh_keys, fresh_values, lengths, step_now):
    robots_here, head_count, head_size = queries.shape
    kv_heads = past_cache.shape[2]
    grouped = queries.reshape(robots_here, kv_heads, head_count // kv_heads, head_size)
    score_scale = 1.0 / math.sqrt(head_size)
    past_scores = (
        jnp.einsum("rkgd,rkcd->rkgc", grouped, past_cache[:, 0], preferred_element_type=jnp.float32)
        * score_scale
    )
    fresh_scores = (
        jnp.einsum("rkgd,rskd->rkgs", grouped, fresh_keys, preferred_element_type=jnp.float32)
        * score_scale
    )
    slot_index = jnp.arange(past_cache.shape[3], dtype=jnp.int32)
    past_scores = jnp.where(
        slot_index[None, None, None, :] < lengths[:, None, None, None], past_scores, -jnp.inf
    )
    turn_index = jnp.arange(fresh_keys.shape[1], dtype=jnp.int32)
    fresh_scores = jnp.where(turn_index[None, None, None, :] <= step_now, fresh_scores, -jnp.inf)
    peak_score = jnp.maximum(jnp.max(past_scores, axis=-1), jnp.max(fresh_scores, axis=-1))
    past_exp = jnp.exp(past_scores - peak_score[..., None])
    fresh_exp = jnp.exp(fresh_scores - peak_score[..., None])
    denominator = jnp.sum(past_exp, axis=-1) + jnp.sum(fresh_exp, axis=-1)
    past_weights = (past_exp / denominator[..., None]).astype(jnp.bfloat16)
    fresh_weights = (fresh_exp / denominator[..., None]).astype(jnp.bfloat16)
    context = jnp.einsum(
        "rkgc,rkcd->rkgd", past_weights, past_cache[:, 1], preferred_element_type=jnp.float32
    )
    context = context + jnp.einsum(
        "rkgs,rskd->rkgd", fresh_weights, fresh_values, preferred_element_type=jnp.float32
    )
    return context.reshape(robots_here, head_count * head_size).astype(jnp.bfloat16)


def local(
    residual, norm_gain, query_weight, key_weight, value_weight, output_weight, past_cache, lengths
):
    group_size = lax.axis_size("wide")
    robots_here, width = residual.shape
    query_cols = query_weight.shape[1]
    kv_cols = key_weight.shape[1]
    fresh_keys = jnp.zeros((robots_here, STEPS, KVH, HD), jnp.bfloat16)
    fresh_values = jnp.zeros((robots_here, STEPS, KVH, HD), jnp.bfloat16)
    final_state = residual
    for step_now in range(STEPS):
        widened = final_state.astype(jnp.float32)
        inverse_rms = lax.rsqrt(jnp.sum(widened * widened, axis=1) / width + norm_eps)
        normed = (widened * inverse_rms[:, None] * norm_gain[None, :]).astype(jnp.bfloat16)
        project_segment = lax.all_gather(normed, "wide", axis=0, tiled=True)
        projected = jnp.concatenate(
            [
                jnp.dot(project_segment, query_weight, preferred_element_type=jnp.float32),
                jnp.dot(project_segment, key_weight, preferred_element_type=jnp.float32),
                jnp.dot(project_segment, value_weight, preferred_element_type=jnp.float32),
            ],
            axis=1,
        ).astype(jnp.bfloat16)
        attend_fresh_keys = fresh_keys
        attend_fresh_values = fresh_values
        arrived = lax.all_to_all(projected, "wide", split_axis=0, concat_axis=1, tiled=True)
        blocks = arrived.reshape(robots_here, group_size, query_cols + 2 * kv_cols)
        positions = lengths + step_now
        queries = rotate_heads(blocks[:, :, :query_cols].reshape(robots_here, QH, HD), positions)
        new_keys = rotate_heads(
            blocks[:, :, query_cols : query_cols + kv_cols].reshape(robots_here, KVH, HD), positions
        )
        new_values = blocks[:, :, query_cols + kv_cols :].reshape(robots_here, KVH, HD)
        attend_fresh_keys = attend_fresh_keys.at[:, step_now].set(new_keys)
        attend_fresh_values = attend_fresh_values.at[:, step_now].set(new_values)
        context = attend_local(
            queries, past_cache, attend_fresh_keys, attend_fresh_values, lengths, step_now
        )
        attended = jnp.dot(
            lax.all_gather(context, "wide", axis=0, tiled=True),
            output_weight,
            preferred_element_type=jnp.float32,
        ).astype(jnp.bfloat16)
        attended, fresh_keys, fresh_values = (attended, attend_fresh_keys, attend_fresh_values)
        returned = lax.all_to_all(attended, "wide", split_axis=0, concat_axis=1, tiled=True)
        final_state = (final_state.astype(jnp.float32) + returned.astype(jnp.float32)).astype(
            jnp.bfloat16
        )
    new_entries = jnp.concatenate(
        [
            fresh_keys.reshape(robots_here, STEPS, KVH * HD),
            fresh_values.reshape(robots_here, STEPS, KVH * HD),
        ],
        axis=2,
    )
    return (final_state, new_entries)


CHUNKS = 2


def copy_to(src, dst, send_sem, recv_sem, peer):
    return pltpu.make_async_remote_copy(
        src_ref=src,
        dst_ref=dst,
        send_sem=send_sem,
        recv_sem=recv_sem,
        device_id={"wide": peer},
        device_id_type=pl.DeviceIdType.MESH,
    )


def exchange_start(n, me, src, dst, send, recv):
    def go(o, _):
        peer = lax.rem(me + o, n)
        copy_to(src.at[peer], dst.at[me], send.at[o], recv.at[o], peer).start()
        return 0

    lax.fori_loop(1, n, go, 0)
    dst[me] = src[me]


def exchange_finish(n, me, src, dst, send, recv):
    def go(o, _):
        peer = lax.rem(me + o, n)
        copy = copy_to(src.at[peer], dst.at[lax.rem(me + n - o, n)], send.at[o], recv.at[o], peer)
        copy.wait_recv()
        copy.wait_send()
        return 0

    lax.fori_loop(1, n, go, 0)


def ring_index(n, position, core):
    depth = n // 4
    y = position // depth
    z = position + y * (2 * depth - 1 - 2 * position)
    return (z * 2 + y) * 2 + core


def ring_gather(n, me, buf, sems):
    send, recv, pair_send, pair_recv = sems
    chips = n // 2
    depth = n // 4
    half = chips // 2
    core = lax.rem(me, 2)
    chip = me // 2
    y = lax.rem(chip, 2)
    z = chip // 2
    place = z + y * (2 * depth - 1 - 2 * z)
    sibling = me + 1 - 2 * core
    rows = buf.shape[1] // CHUNKS

    def at(position):
        return ring_index(n, lax.rem(position + 2 * chips, chips), core)

    def piece(slot, c):
        return buf.at[slot, pl.ds(c * rows, rows)]

    def hop(way, h, c):
        step = 1 if way == 0 else -1
        slot = at(place - step * h)
        return copy_to(
            piece(slot, c), piece(slot, c), send.at[way, h, c], recv.at[way, h, c], at(place + step)
        )

    def valid(way, h, c):
        return h < half - 1 or (h == half - 1 and c % 2 == way)

    def pair(way, h, c):
        step = 1 if way == 0 else -1
        slot = at(place - step * h)
        return copy_to(
            piece(slot, c), piece(slot, c), pair_send.at[way, h, c], pair_recv.at[way, h, c], sibling
        )

    started, pairs = [], []
    for c in range(CHUNKS):
        for way in (0, 1):
            copy = hop(way, 0, c)
            copy.start()
            started.append(copy)
    for c in range(CHUNKS):
        copy = pair(0, 0, c)
        copy.start()
        pairs.append(copy)
    for h in range(half):
        for c in range(CHUNKS):
            for way in (0, 1):
                if not valid(way, h, c):
                    continue
                hop(way, h, c).wait_recv()
                if valid(way, h + 1, c):
                    copy = hop(way, h + 1, c)
                    copy.start()
                    started.append(copy)
                copy = pair(way, h + 1, c)
                copy.start()
                pairs.append(copy)
    for copy in pairs:
        copy.wait_recv()
    for copy in started + pairs:
        copy.wait_send()


def layer_kernel(
    n,
    x0_ref, gain_ref, freq_ref, lengths_ref, wq_hbm, wk_hbm, wv_hbm, wo_hbm, cache_hbm,
    out_ref, keys_ref, values_ref,
    w_ref, wk_ref, wv_ref, wo_ref, cache_ref, xr_ref, xc_ref, xg_ref, pr_ref, m32_ref, sbuf_ref,
    rbuf_ref, cos_ref, sin_ref, rq_ref, cg_ref, t32_ref, acc_ref, fbuf_ref, fr_ref,
    load_sem, x_send, x_recv, q_send, q_recv, f_send, f_recv,
    g_send, g_recv, gp_send, gp_recv, c_send, c_recv, cp_send, cp_recv,
):
    me = lax.axis_index("wide")
    robots = lengths_ref.shape[0]
    rows = n * robots
    width = w_ref.shape[0]
    loads = [
        pltpu.make_async_copy(wk_hbm, wk_ref, load_sem.at[0]),
        pltpu.make_async_copy(wv_hbm, wv_ref, load_sem.at[1]),
        pltpu.make_async_copy(wq_hbm, w_ref.at[:, pl.ds(0, 512)], load_sem.at[2]),
        pltpu.make_async_copy(cache_hbm, cache_ref, load_sem.at[3]),
        pltpu.make_async_copy(wo_hbm, wo_ref, load_sem.at[4]),
    ]
    for load in loads:
        load.start()
    barrier = pltpu.get_barrier_semaphore()

    def greet(o, _):
        pl.semaphore_signal(
            barrier, inc=1, device_id={"wide": lax.rem(me + o, n)}, device_id_type=pl.DeviceIdType.MESH
        )
        return 0

    lax.fori_loop(1, n, greet, 0)
    pl.semaphore_wait(barrier, n - 1)
    exchange_start(n, me, x0_ref, xr_ref, x_send, x_recv)

    robot_of = lax.broadcasted_iota(jnp.int32, (32, 128), 0) % robots
    lane = lax.broadcasted_iota(jnp.int32, (32, 128), 1)
    length = jnp.zeros((32, 128), jnp.int32)
    for r in range(robots):
        length = jnp.where(robot_of == r, lengths_ref[r], length)
    for t in range(STEPS):
        angles = (length + t).astype(jnp.float32) * freq_ref[...]
        cos_ref[t] = jnp.cos(angles)
        sine = jnp.sin(angles)
        sin_ref[t] = jnp.where(lane < HD // 2, -sine, sine)
    m32_ref[...] = jnp.zeros_like(m32_ref)
    keys_ref[...] = jnp.zeros_like(keys_ref)
    values_ref[...] = jnp.zeros_like(values_ref)

    loads[0].wait()
    loads[1].wait()

    def join(i, _):
        part = pl.ds(pl.multiple_of(i * 512, 512), 512)
        w_ref[part, 512:640] = jnp.concatenate([wk_ref[part, :], wv_ref[part, :]], axis=1)
        return 0

    lax.fori_loop(0, width // 512, join, 0)
    exchange_finish(n, me, x0_ref, xr_ref, x_send, x_recv)
    t32_ref[0:256] = xr_ref[...].reshape(256, 128).astype(jnp.float32)
    for j in range(4):
        for r in range(robots):
            xc_ref[pl.ds(rows * j + r, n, stride=robots), :] = t32_ref[
                pl.ds(4 * j + r, n, stride=16), :
            ]
    loads[2].wait()

    def step(t, _):
        xg_ref[me] = xc_ref[...].astype(jnp.bfloat16)
        ring_gather(n, me, xg_ref, (g_send, g_recv, gp_send, gp_recv))

        def square(s, total):
            x = xg_ref[s].astype(jnp.float32)
            x = x * x
            for j in range(4):
                total = total + x[rows * j : rows * j + rows]
            return total

        total = lax.fori_loop(0, n, square, jnp.zeros((rows, 128), jnp.float32))
        inverse = lax.rsqrt(jnp.sum(total, axis=1, keepdims=True) / width + norm_eps)
        inverse = jnp.broadcast_to(inverse, (rows, 128))
        acc_ref[...] = jnp.zeros_like(acc_ref)

        def project(s, _):
            parts = []
            for j in range(4):
                x = xg_ref[s, rows * j : rows * j + rows].astype(jnp.float32)
                parts.append((x * inverse * gain_ref[pl.ds(4 * s + j, 1), :]).astype(jnp.bfloat16))
            acc_ref[...] += jnp.dot(
                jnp.concatenate(parts, axis=1),
                w_ref[pl.ds(pl.multiple_of(s * 512, 512), 512), :],
                preferred_element_type=jnp.float32,
            )
            return 0

        lax.fori_loop(0, n, project, 0)
        for j in range(5):
            pr_ref[rows * j : rows * j + rows] = acc_ref[:, 128 * j : 128 * j + 128]
        for j in range(5):
            for r in range(robots):
                m32_ref[pl.ds(4 * j + r, n, stride=32), :] = pr_ref[
                    pl.ds(rows * j + r, n, stride=robots), :
                ]
        sbuf_ref[...] = m32_ref[...].reshape(n, 32, 128).astype(jnp.bfloat16)
        exchange_start(n, me, sbuf_ref, rbuf_ref, q_send, q_recv)

        @pl.when(t == 0)
        def _():
            loads[3].wait()

        exchange_finish(n, me, sbuf_ref, rbuf_ref, q_send, q_recv)
        cosine = cos_ref[t]
        sine = sin_ref[t]
        slot = lax.broadcasted_iota(jnp.int32, (8, 512), 1)
        low = lax.broadcasted_iota(jnp.int32, (8, 128), 1) < HD // 2
        scale = 1.0 / math.sqrt(HD)

        def attend(g, _):
            first = rbuf_ref[2 * g].astype(jnp.float32)
            second = rbuf_ref[2 * g + 1].astype(jnp.float32)
            q = jnp.concatenate([first[:16], second[:16]], axis=0)
            q = q * cosine + pltpu.roll(q, HD // 2, 1) * sine
            rq_ref[...] = q.astype(jnp.bfloat16).astype(jnp.float32)
            a, b = first[16:24], second[16:24]
            k = jnp.where(low, a, pltpu.roll(b, HD // 2, 1))
            v = jnp.where(low, pltpu.roll(a, HD // 2, 1), b)
            k = k * cosine[:8] + pltpu.roll(k, HD // 2, 1) * sine[:8]
            keys_ref[t, g] = k.astype(jnp.bfloat16).astype(jnp.float32)
            values_ref[t, g] = v
            past, fresh = [], []
            for r in range(robots):
                q = rq_ref[pl.ds(r, 8, stride=robots), :]
                s = lax.dot_general(
                    q.astype(jnp.bfloat16),
                    cache_ref[r, 0, g],
                    (((1,), (1,)), ((), ())),
                    preferred_element_type=jnp.float32,
                )
                past.append(jnp.where(slot < lengths_ref[r], s * scale, -jnp.inf))
                fresh.append(
                    [
                        jnp.sum(q * keys_ref[i, g, r : r + 1, :], axis=1, keepdims=True) * scale
                        for i in range(STEPS)
                    ]
                )
            past = jnp.concatenate(past, axis=0)
            fresh = [jnp.concatenate([f[i] for f in fresh], axis=0) for i in range(STEPS)]
            for i in range(1, STEPS):
                fresh[i] = jnp.where(i <= t, fresh[i], -jnp.inf)
            peak = jnp.max(past, axis=1, keepdims=True)
            for f in fresh:
                peak = jnp.maximum(peak, f)
            past = jnp.exp(past - peak)
            fresh = [jnp.exp(f - peak) for f in fresh]
            denominator = jnp.sum(past, axis=1, keepdims=True)
            for f in fresh:
                denominator = denominator + f
            past = past / denominator
            fresh = [(f / denominator).astype(jnp.bfloat16).astype(jnp.float32) for f in fresh]
            context = []
            for r in range(robots):
                c = jnp.dot(
                    past[8 * r : 8 * r + 8].astype(jnp.bfloat16),
                    cache_ref[r, 1, g],
                    preferred_element_type=jnp.float32,
                )
                for i in range(STEPS):
                    c = c + fresh[i][8 * r : 8 * r + 8] * values_ref[i, g, r : r + 1, :]
                context.append(c)
            cg_ref[me, pl.ds(pl.multiple_of(g * 32, 32), 32), :] = jnp.concatenate(
                context, axis=0
            ).astype(jnp.bfloat16)
            return 0

        lax.fori_loop(0, KVH, attend, 0)

        @pl.when(t == 0)
        def _():
            loads[4].wait()

        ring_gather(n, me, cg_ref, (c_send, c_recv, cp_send, cp_recv))
        acc_ref[...] = jnp.zeros_like(acc_ref)

        def output(g, _):
            block = cg_ref[:, pl.ds(pl.multiple_of(g * 32, 32), 32), :]
            t32_ref[...] = block.reshape(n * 32, 128).astype(jnp.float32)
            left = jnp.concatenate(
                [t32_ref[pl.ds(h, rows, stride=8), :].astype(jnp.bfloat16) for h in range(8)], axis=1
            )
            acc_ref[:, 0:512] += jnp.dot(
                left,
                wo_ref[pl.ds(pl.multiple_of(g * 1024, 1024), 1024), :],
                preferred_element_type=jnp.float32,
            )
            return 0

        lax.fori_loop(0, KVH, output, 0)
        for j in range(4):
            part = slice(rows * j, rows * j + rows)
            attended = acc_ref[:, 128 * j : 128 * j + 128].astype(jnp.bfloat16).astype(jnp.float32)
            xc_ref[part] = (xc_ref[part] + attended).astype(jnp.bfloat16).astype(jnp.float32)
        return 0

    lax.fori_loop(0, STEPS, step, 0)
    for j in range(4):
        for r in range(robots):
            t32_ref[pl.ds(4 * j + r, n, stride=16), :] = xc_ref[
                pl.ds(rows * j + r, n, stride=robots), :
            ]
    fbuf_ref[...] = t32_ref[0:256].reshape(n, 16, 128).astype(jnp.bfloat16)
    exchange_start(n, me, fbuf_ref, fr_ref, f_send, f_recv)
    exchange_finish(n, me, fbuf_ref, fr_ref, f_send, f_recv)
    t32_ref[0:256] = fr_ref[...].reshape(256, 128).astype(jnp.float32)
    for r in range(robots):
        out_ref[64 * r : 64 * r + 64] = t32_ref[pl.ds(r, 64, stride=robots), :].astype(jnp.bfloat16)


def fused(
    residual, norm_gain, query_weight, key_weight, value_weight, output_weight, past_cache, lengths
):
    n = lax.axis_size("wide")
    robots, width = residual.shape
    frequency = rope_base ** (-2.0 * jnp.arange(HD // 2, dtype=jnp.float32) / HD)
    frequency = jnp.concatenate([frequency, frequency])[None, :]
    x0 = residual.reshape(robots, n, 4, 128).transpose(1, 2, 0, 3).reshape(n, 16, 128)
    vmem = pl.BlockSpec(memory_space=pltpu.VMEM)
    smem = pl.BlockSpec(memory_space=pltpu.SMEM)
    any_spec = pl.BlockSpec(memory_space=pl.ANY)
    bf16, f32 = jnp.bfloat16, jnp.float32
    dma = pltpu.SemaphoreType.DMA
    half = n // 4
    ring_sems = [
        dma((2, half, CHUNKS)),
        dma((2, half, CHUNKS)),
        dma((2, half + 1, CHUNKS)),
        dma((2, half + 1, CHUNKS)),
    ]
    out, keys, values = pl.pallas_call(
        partial(layer_kernel, n),
        out_shape=(
            jax.ShapeDtypeStruct((robots * 64, 128), bf16),
            jax.ShapeDtypeStruct((STEPS, KVH, 8, HD), f32),
            jax.ShapeDtypeStruct((STEPS, KVH, 8, HD), f32),
        ),
        in_specs=[vmem, vmem, vmem, smem] + [any_spec] * 5,
        out_specs=(vmem, vmem, vmem),
        scratch_shapes=[
            pltpu.VMEM((width, 640), bf16),
            pltpu.VMEM(key_weight.shape, bf16),
            pltpu.VMEM(value_weight.shape, bf16),
            pltpu.VMEM(output_weight.shape, bf16),
            pltpu.VMEM(past_cache.shape, bf16),
            pltpu.VMEM((n, 16, 128), bf16),
            pltpu.VMEM((n * 16, 128), f32),
            pltpu.VMEM((n, n * 16, 128), bf16),
            pltpu.VMEM((5 * n * robots, 128), f32),
            pltpu.VMEM((n * 32, 128), f32),
            pltpu.VMEM((n, 32, 128), bf16),
            pltpu.VMEM((n, 32, 128), bf16),
            pltpu.VMEM((STEPS, 32, 128), f32),
            pltpu.VMEM((STEPS, 32, 128), f32),
            pltpu.VMEM((32, 128), f32),
            pltpu.VMEM((n, KVH * 32, 128), bf16),
            pltpu.VMEM((n * 32, 128), f32),
            pltpu.VMEM((n * robots, 640), f32),
            pltpu.VMEM((n, 16, 128), bf16),
            pltpu.VMEM((n, 16, 128), bf16),
            dma((5,)),
            dma((n,)), dma((n,)), dma((n,)), dma((n,)), dma((n,)), dma((n,)),
        ]
        + ring_sems
        + ring_sems,
        compiler_params=pltpu.CompilerParams(
            collective_id=0, has_side_effects=True, vmem_limit_bytes=58 * 1024 * 1024
        ),
    )(
        x0, norm_gain.reshape(width // 128, 128), frequency, lengths,
        query_weight, key_weight, value_weight, output_weight, past_cache,
    )
    entries = jnp.stack([keys[:, :, :robots], values[:, :, :robots]], axis=1)
    entries = entries.transpose(3, 0, 1, 2, 4).reshape(robots, STEPS, 2 * KVH * HD)
    return out.reshape(robots, width), entries.astype(bf16)


def dispatch(*arrays):
    residual, _, query_weight, key_weight, _, _, past_cache, _ = arrays
    fits = (
        lax.axis_size("wide") == 16
        and residual.shape == (4, 8192)
        and query_weight.shape[1] == 512
        and key_weight.shape[1] == 64
        and past_cache.shape[1:] == (2, KVH, 512, HD)
    )
    return fused(*arrays) if fits else local(*arrays)


def solution(mesh):
    return jax.shard_map(
        dispatch,
        mesh=mesh,
        in_specs=(
            P(("groups", "wide"), None),
            P(),
            P(None, "wide"),
            P(None, "wide"),
            P(None, "wide"),
            P(None, "wide"),
            P(("groups", "wide"), None, None, None, None),
            P(("groups", "wide")),
        ),
        out_specs=(P(("groups", "wide"), None), P(("groups", "wide"), None, None)),
        check_vma=False,
    )
```

```python
import math
from functools import partial

import jax
import jax.numpy as jnp
import numpy as np
from jax import lax
from jax.experimental import pallas as pl
from jax.experimental.pallas import tpu as pltpu
from jax.sharding import PartitionSpec as P

QH = 64
KVH = 8
HD = 128
STEPS = 2


rope_base = 500000.0
norm_eps = 1e-05


def rotate_heads(heads_block, positions):
    head_size = heads_block.shape[-1]
    half_size = head_size // 2
    frequency = rope_base ** (-2.0 * jnp.arange(half_size, dtype=jnp.float32) / head_size)
    angles = positions.astype(jnp.float32)[:, None, None] * frequency[None, None, :]
    cosine = jnp.cos(angles)
    sine_part = jnp.sin(angles)
    values = heads_block.astype(jnp.float32)
    first_half = values[..., :half_size]
    second = values[..., half_size:]
    return jnp.concatenate(
        [first_half * cosine - second * sine_part, second * cosine + first_half * sine_part],
        axis=-1,
    ).astype(jnp.bfloat16)


def attend_local(queries, past_cache, fresh_keys, fresh_values, lengths, step_now):
    robots_here, head_count, head_size = queries.shape
    kv_heads = past_cache.shape[2]
    grouped = queries.reshape(robots_here, kv_heads, head_count // kv_heads, head_size)
    score_scale = 1.0 / math.sqrt(head_size)
    past_scores = (
        jnp.einsum("rkgd,rkcd->rkgc", grouped, past_cache[:, 0], preferred_element_type=jnp.float32)
        * score_scale
    )
    fresh_scores = (
        jnp.einsum("rkgd,rskd->rkgs", grouped, fresh_keys, preferred_element_type=jnp.float32)
        * score_scale
    )
    slot_index = jnp.arange(past_cache.shape[3], dtype=jnp.int32)
    past_scores = jnp.where(
        slot_index[None, None, None, :] < lengths[:, None, None, None], past_scores, -jnp.inf
    )
    turn_index = jnp.arange(fresh_keys.shape[1], dtype=jnp.int32)
    fresh_scores = jnp.where(turn_index[None, None, None, :] <= step_now, fresh_scores, -jnp.inf)
    peak_score = jnp.maximum(jnp.max(past_scores, axis=-1), jnp.max(fresh_scores, axis=-1))
    past_exp = jnp.exp(past_scores - peak_score[..., None])
    fresh_exp = jnp.exp(fresh_scores - peak_score[..., None])
    denominator = jnp.sum(past_exp, axis=-1) + jnp.sum(fresh_exp, axis=-1)
    past_weights = (past_exp / denominator[..., None]).astype(jnp.bfloat16)
    fresh_weights = (fresh_exp / denominator[..., None]).astype(jnp.bfloat16)
    context = jnp.einsum(
        "rkgc,rkcd->rkgd", past_weights, past_cache[:, 1], preferred_element_type=jnp.float32
    )
    context = context + jnp.einsum(
        "rkgs,rskd->rkgd", fresh_weights, fresh_values, preferred_element_type=jnp.float32
    )
    return context.reshape(robots_here, head_count * head_size).astype(jnp.bfloat16)


def local(
    residual, norm_gain, query_weight, key_weight, value_weight, output_weight, past_cache, lengths
):
    group_size = lax.axis_size("wide")
    robots_here, width = residual.shape
    query_cols = query_weight.shape[1]
    kv_cols = key_weight.shape[1]
    fresh_keys = jnp.zeros((robots_here, STEPS, KVH, HD), jnp.bfloat16)
    fresh_values = jnp.zeros((robots_here, STEPS, KVH, HD), jnp.bfloat16)
    final_state = residual
    for step_now in range(STEPS):
        widened = final_state.astype(jnp.float32)
        inverse_rms = lax.rsqrt(jnp.sum(widened * widened, axis=1) / width + norm_eps)
        normed = (widened * inverse_rms[:, None] * norm_gain[None, :]).astype(jnp.bfloat16)
        project_segment = lax.all_gather(normed, "wide", axis=0, tiled=True)
        projected = jnp.concatenate(
            [
                jnp.dot(project_segment, query_weight, preferred_element_type=jnp.float32),
                jnp.dot(project_segment, key_weight, preferred_element_type=jnp.float32),
                jnp.dot(project_segment, value_weight, preferred_element_type=jnp.float32),
            ],
            axis=1,
        ).astype(jnp.bfloat16)
        attend_fresh_keys = fresh_keys
        attend_fresh_values = fresh_values
        arrived = lax.all_to_all(projected, "wide", split_axis=0, concat_axis=1, tiled=True)
        blocks = arrived.reshape(robots_here, group_size, query_cols + 2 * kv_cols)
        positions = lengths + step_now
        queries = rotate_heads(blocks[:, :, :query_cols].reshape(robots_here, QH, HD), positions)
        new_keys = rotate_heads(
            blocks[:, :, query_cols : query_cols + kv_cols].reshape(robots_here, KVH, HD), positions
        )
        new_values = blocks[:, :, query_cols + kv_cols :].reshape(robots_here, KVH, HD)
        attend_fresh_keys = attend_fresh_keys.at[:, step_now].set(new_keys)
        attend_fresh_values = attend_fresh_values.at[:, step_now].set(new_values)
        context = attend_local(
            queries, past_cache, attend_fresh_keys, attend_fresh_values, lengths, step_now
        )
        attended = jnp.dot(
            lax.all_gather(context, "wide", axis=0, tiled=True),
            output_weight,
            preferred_element_type=jnp.float32,
        ).astype(jnp.bfloat16)
        attended, fresh_keys, fresh_values = (attended, attend_fresh_keys, attend_fresh_values)
        returned = lax.all_to_all(attended, "wide", split_axis=0, concat_axis=1, tiled=True)
        final_state = (final_state.astype(jnp.float32) + returned.astype(jnp.float32)).astype(
            jnp.bfloat16
        )
    new_entries = jnp.concatenate(
        [
            fresh_keys.reshape(robots_here, STEPS, KVH * HD),
            fresh_values.reshape(robots_here, STEPS, KVH * HD),
        ],
        axis=2,
    )
    return (final_state, new_entries)


def copy_to(src, dst, send_sem, recv_sem, peer):
    return pltpu.make_async_remote_copy(
        src_ref=src,
        dst_ref=dst,
        send_sem=send_sem,
        recv_sem=recv_sem,
        device_id={"wide": peer},
        device_id_type=pl.DeviceIdType.MESH,
    )


def exchange_start(n, me, src, dst, send, recv):
    def go(o, _):
        peer = lax.rem(me + o, n)
        copy_to(src.at[peer], dst.at[me], send.at[o], recv.at[o], peer).start()
        return 0

    lax.fori_loop(1, n, go, 0)
    dst[me] = src[me]


def exchange_finish(n, me, src, dst, send, recv):
    def go(o, _):
        peer = lax.rem(me + o, n)
        copy = copy_to(src.at[peer], dst.at[lax.rem(me + n - o, n)], send.at[o], recv.at[o], peer)
        copy.wait_recv()
        copy.wait_send()
        return 0

    lax.fori_loop(1, n, go, 0)


PIECES = 4
LAG = 2


class Gather:
    def __init__(self, n, me, buf, sems, pieces):
        self.n, self.me, self.buf = n, me, buf
        self.send, self.recv, self.pair_send, self.pair_recv = sems
        self.chips = n // 2
        self.rows = buf.shape[1] // pieces
        self.order = sorted(range(1, self.chips), key=lambda o: min(o, self.chips - o))

    def part(self, slot, c):
        return self.buf.at[slot, pl.ds(pl.multiple_of(c * self.rows, self.rows), self.rows)]

    def far(self, o, c):
        part = self.part(self.me, c)
        peer = lax.rem(self.me + 2 * o, self.n)
        return copy_to(part, part, self.send.at[c, o], self.recv.at[c, o], peer)

    def near(self, o, c):
        part = self.part(lax.rem(self.me + self.n - 2 * o, self.n), c)
        sibling = self.me + 1 - 2 * lax.rem(self.me, 2)
        return copy_to(part, part, self.pair_send.at[c, o], self.pair_recv.at[c, o], sibling)

    def start(self, c):
        for o in self.order[::-1]:
            self.far(o, c).start()
        self.near(0, c).start()

    def forward(self, c):
        for o in self.order:
            self.far(o, c).wait_recv()
            self.near(o, c).start()

    def arrive(self, c):
        for o in range(self.chips):
            self.near(o, c).wait_recv()

    def drain(self, c):
        self.near(0, c).wait_send()
        for o in self.order:
            self.far(o, c).wait_send()
            self.near(o, c).wait_send()


def layer_kernel(
    n,
    x0_ref, gain_ref, freq_ref, lengths_ref, wq_hbm, wk_hbm, wv_hbm, wo_hbm, cache_hbm,
    out_ref, keys_ref, values_ref,
    wq_ref, wkv_ref, wo_ref, cache_ref, xr_ref, xc_ref, xg_ref, pr_ref, m32_ref, sbuf_ref,
    rbuf_ref, cos_ref, sin_ref, rq_ref, cg_ref, t32_ref, acc_ref, fbuf_ref, fr_ref,
    load_sem, x_send, x_recv, q_send, q_recv, f_send, f_recv,
    *gather_sems,
):
    me = lax.axis_index("wide")
    robots = lengths_ref.shape[0]
    rows = n * robots
    width = wq_ref.shape[0]
    loads = [
        pltpu.make_async_copy(wk_hbm, wkv_ref.at[pl.ds(0, 64)], load_sem.at[0]),
        pltpu.make_async_copy(wv_hbm, wkv_ref.at[pl.ds(64, 64)], load_sem.at[1]),
        pltpu.make_async_copy(wq_hbm, wq_ref, load_sem.at[2]),
        pltpu.make_async_copy(cache_hbm, cache_ref, load_sem.at[3]),
        pltpu.make_async_copy(wo_hbm, wo_ref, load_sem.at[4]),
    ]
    for load in loads:
        load.start()
    barrier = pltpu.get_barrier_semaphore()

    def greet(o, _):
        pl.semaphore_signal(
            barrier, inc=1, device_id={"wide": lax.rem(me + o, n)}, device_id_type=pl.DeviceIdType.MESH
        )
        return 0

    lax.fori_loop(1, n, greet, 0)
    for k in range(4 * n):
        t32_ref[4 * k : 4 * k + 4] = x0_ref[:, 128 * k : 128 * k + 128].astype(jnp.float32)
    fbuf_ref[...] = t32_ref[0:256].reshape(n, 16, 128).astype(jnp.bfloat16)
    pl.semaphore_wait(barrier, n - 1)
    exchange_start(n, me, fbuf_ref, xr_ref, x_send, x_recv)

    robot_of = lax.broadcasted_iota(jnp.int32, (32, 128), 0) % robots
    lane = lax.broadcasted_iota(jnp.int32, (32, 128), 1)
    length = jnp.zeros((32, 128), jnp.int32)
    for r in range(robots):
        length = jnp.where(robot_of == r, lengths_ref[r], length)
    for t in range(STEPS):
        angles = (length + t).astype(jnp.float32) * freq_ref[...]
        cos_ref[t] = jnp.cos(angles)
        sine = jnp.sin(angles)
        sin_ref[t] = jnp.where(lane < HD // 2, -sine, sine)
    m32_ref[...] = jnp.zeros_like(m32_ref)
    keys_ref[...] = jnp.zeros_like(keys_ref)
    values_ref[...] = jnp.zeros_like(values_ref)

    exchange_finish(n, me, fbuf_ref, xr_ref, x_send, x_recv)
    t32_ref[0:256] = xr_ref[...].reshape(256, 128).astype(jnp.float32)
    for j in range(4):
        for r in range(robots):
            xc_ref[pl.ds(rows * j + r, n, stride=robots), :] = t32_ref[
                pl.ds(4 * j + r, n, stride=16), :
            ]
    for load in loads[:3]:
        load.wait()

    columns = Gather(n, me, xg_ref, gather_sems[:4], 1)
    contexts = Gather(n, me, cg_ref, gather_sems[4:], PIECES)

    def step(t, _):
        xg_ref[me] = xc_ref[...].astype(jnp.bfloat16)
        columns.start(0)
        columns.forward(0)
        columns.arrive(0)

        def square(s, total):
            x = xg_ref[s].astype(jnp.float32)
            x = x * x
            for j in range(4):
                total = total + x[rows * j : rows * j + rows]
            return total

        total = lax.fori_loop(0, n, square, jnp.zeros((rows, 128), jnp.float32))
        inverse = lax.rsqrt(jnp.sum(total, axis=1, keepdims=True) / width + norm_eps)
        inverse = jnp.broadcast_to(inverse, (rows, 128))
        acc_ref[...] = jnp.zeros_like(acc_ref)

        def project(s, _):
            parts = []
            for j in range(4):
                x = xg_ref[s, rows * j : rows * j + rows].astype(jnp.float32)
                parts.append((x * inverse * gain_ref[pl.ds(4 * s + j, 1), :]).astype(jnp.bfloat16))
            normed = jnp.concatenate(parts, axis=1)
            part = pl.ds(pl.multiple_of(s * 512, 512), 512)
            acc_ref[:, 0:512] += jnp.dot(
                normed, wq_ref[part, :], preferred_element_type=jnp.float32
            )
            acc_ref[:, 512:640] += lax.dot_general(
                normed,
                wkv_ref[:, part],
                (((1,), (1,)), ((), ())),
                preferred_element_type=jnp.float32,
            )
            return 0

        lax.fori_loop(0, n, project, 0)
        for j in range(5):
            pr_ref[rows * j : rows * j + rows] = acc_ref[:, 128 * j : 128 * j + 128]
        for j in range(5):
            for r in range(robots):
                m32_ref[pl.ds(4 * j + r, n, stride=32), :] = pr_ref[
                    pl.ds(rows * j + r, n, stride=robots), :
                ]
        sbuf_ref[...] = m32_ref[...].reshape(n, 32, 128).astype(jnp.bfloat16)
        exchange_start(n, me, sbuf_ref, rbuf_ref, q_send, q_recv)

        @pl.when(t == 0)
        def _():
            loads[3].wait()

        columns.drain(0)
        exchange_finish(n, me, sbuf_ref, rbuf_ref, q_send, q_recv)
        cosine = cos_ref[t]
        sine = sin_ref[t]
        slot = lax.broadcasted_iota(jnp.int32, (8, 512), 1)
        low = lax.broadcasted_iota(jnp.int32, (8, 128), 1) < HD // 2
        scale = 1.0 / math.sqrt(HD)

        def attend(g, _):
            first = rbuf_ref[2 * g].astype(jnp.float32)
            second = rbuf_ref[2 * g + 1].astype(jnp.float32)
            q = jnp.concatenate([first[:16], second[:16]], axis=0)
            q = q * cosine + pltpu.roll(q, HD // 2, 1) * sine
            rq_ref[...] = q.astype(jnp.bfloat16).astype(jnp.float32)
            a, b = first[16:24], second[16:24]
            k = jnp.where(low, a, pltpu.roll(b, HD // 2, 1))
            v = jnp.where(low, pltpu.roll(a, HD // 2, 1), b)
            k = k * cosine[:8] + pltpu.roll(k, HD // 2, 1) * sine[:8]
            keys_ref[t, g] = k.astype(jnp.bfloat16).astype(jnp.float32)
            values_ref[t, g] = v
            past, fresh = [], []
            for r in range(robots):
                q = rq_ref[pl.ds(r, 8, stride=robots), :]
                s = lax.dot_general(
                    q.astype(jnp.bfloat16),
                    cache_ref[r, 0, g],
                    (((1,), (1,)), ((), ())),
                    preferred_element_type=jnp.float32,
                )
                past.append(jnp.where(slot < lengths_ref[r], s * scale, -jnp.inf))
                fresh.append(
                    [
                        jnp.sum(q * keys_ref[i, g, r : r + 1, :], axis=1, keepdims=True) * scale
                        for i in range(STEPS)
                    ]
                )
            past = jnp.concatenate(past, axis=0)
            fresh = [jnp.concatenate([f[i] for f in fresh], axis=0) for i in range(STEPS)]
            for i in range(1, STEPS):
                fresh[i] = jnp.where(i <= t, fresh[i], -jnp.inf)
            peak = jnp.max(past, axis=1, keepdims=True)
            for f in fresh:
                peak = jnp.maximum(peak, f)
            past = jnp.exp(past - peak)
            fresh = [jnp.exp(f - peak) for f in fresh]
            denominator = jnp.sum(past, axis=1, keepdims=True)
            for f in fresh:
                denominator = denominator + f
            past = past / denominator
            fresh = [(f / denominator).astype(jnp.bfloat16).astype(jnp.float32) for f in fresh]
            context = []
            for r in range(robots):
                c = jnp.dot(
                    past[8 * r : 8 * r + 8].astype(jnp.bfloat16),
                    cache_ref[r, 1, g],
                    preferred_element_type=jnp.float32,
                )
                for i in range(STEPS):
                    c = c + fresh[i][8 * r : 8 * r + 8] * values_ref[i, g, r : r + 1, :]
                context.append(c)
            cg_ref[me, pl.ds(pl.multiple_of(g * 32, 32), 32), :] = jnp.concatenate(
                context, axis=0
            ).astype(jnp.bfloat16)
            return 0

        each = KVH // PIECES

        def attend_piece(c, _):
            lax.fori_loop(c * each, c * each + each, attend, 0)
            contexts.start(c)

            @pl.when(c >= LAG)
            def _():
                contexts.forward(c - LAG)

            return 0

        lax.fori_loop(0, PIECES, attend_piece, 0)

        @pl.when(t == 0)
        def _():
            loads[4].wait()

        acc_ref[...] = jnp.zeros_like(acc_ref)

        def output(g, _):
            block = cg_ref[:, pl.ds(pl.multiple_of(g * 32, 32), 32), :]
            t32_ref[...] = block.reshape(n * 32, 128).astype(jnp.float32)
            left = jnp.concatenate(
                [t32_ref[pl.ds(h, rows, stride=8), :].astype(jnp.bfloat16) for h in range(8)], axis=1
            )
            acc_ref[:, 0:512] += jnp.dot(
                left,
                wo_ref[pl.ds(pl.multiple_of(g * 1024, 1024), 1024), :],
                preferred_element_type=jnp.float32,
            )
            return 0

        def output_piece(c, _):
            @pl.when(c + PIECES - LAG < PIECES)
            def _():
                contexts.forward(c + PIECES - LAG)

            contexts.arrive(c)
            lax.fori_loop(c * each, c * each + each, output, 0)
            return 0

        lax.fori_loop(0, PIECES, output_piece, 0)
        for j in range(4):
            part = slice(rows * j, rows * j + rows)
            attended = acc_ref[:, 128 * j : 128 * j + 128].astype(jnp.bfloat16).astype(jnp.float32)
            xc_ref[part] = (xc_ref[part] + attended).astype(jnp.bfloat16).astype(jnp.float32)

        def drain(c, _):
            contexts.drain(c)
            return 0

        lax.fori_loop(0, PIECES, drain, 0)
        return 0

    lax.fori_loop(0, STEPS, step, 0)
    for j in range(4):
        for r in range(robots):
            t32_ref[pl.ds(4 * j + r, n, stride=16), :] = xc_ref[
                pl.ds(rows * j + r, n, stride=robots), :
            ]
    fbuf_ref[...] = t32_ref[0:256].reshape(n, 16, 128).astype(jnp.bfloat16)
    exchange_start(n, me, fbuf_ref, fr_ref, f_send, f_recv)
    exchange_finish(n, me, fbuf_ref, fr_ref, f_send, f_recv)
    t32_ref[0:256] = fr_ref[...].reshape(256, 128).astype(jnp.float32)
    for k in range(4 * n):
        out_ref[:, 128 * k : 128 * k + 128] = t32_ref[4 * k : 4 * k + 4].astype(jnp.bfloat16)


def fused(
    residual, norm_gain, query_weight, key_weight, value_weight, output_weight, past_cache, lengths
):
    n = lax.axis_size("wide")
    robots, width = residual.shape
    frequency = np.tile(rope_base ** (-2.0 * np.arange(HD // 2) / HD), 2)
    frequency = jnp.asarray(frequency[None, :], jnp.float32)
    vmem = pl.BlockSpec(memory_space=pltpu.VMEM)
    smem = pl.BlockSpec(memory_space=pltpu.SMEM)
    any_spec = pl.BlockSpec(memory_space=pl.ANY)
    bf16, f32 = jnp.bfloat16, jnp.float32
    dma = pltpu.SemaphoreType.DMA
    gather_sems = [dma((1, n // 2))] * 4 + [dma((PIECES, n // 2))] * 4
    out, keys, values = pl.pallas_call(
        partial(layer_kernel, n),
        out_shape=(
            jax.ShapeDtypeStruct((robots, width), bf16),
            jax.ShapeDtypeStruct((STEPS, KVH, 8, HD), f32),
            jax.ShapeDtypeStruct((STEPS, KVH, 8, HD), f32),
        ),
        in_specs=[vmem, vmem, vmem, smem] + [any_spec] * 5,
        out_specs=(vmem, vmem, vmem),
        scratch_shapes=[
            pltpu.VMEM(query_weight.shape, bf16),
            pltpu.VMEM((2 * key_weight.shape[1], width), bf16),
            pltpu.VMEM(output_weight.shape, bf16),
            pltpu.VMEM(past_cache.shape, bf16),
            pltpu.VMEM((n, 16, 128), bf16),
            pltpu.VMEM((n * 16, 128), f32),
            pltpu.VMEM((n, n * 16, 128), bf16),
            pltpu.VMEM((5 * n * robots, 128), f32),
            pltpu.VMEM((n * 32, 128), f32),
            pltpu.VMEM((n, 32, 128), bf16),
            pltpu.VMEM((n, 32, 128), bf16),
            pltpu.VMEM((STEPS, 32, 128), f32),
            pltpu.VMEM((STEPS, 32, 128), f32),
            pltpu.VMEM((32, 128), f32),
            pltpu.VMEM((n, KVH * 32, 128), bf16),
            pltpu.VMEM((n * 32, 128), f32),
            pltpu.VMEM((n * robots, 640), f32),
            pltpu.VMEM((n, 16, 128), bf16),
            pltpu.VMEM((n, 16, 128), bf16),
            dma((5,)),
            dma((n,)), dma((n,)), dma((n,)), dma((n,)), dma((n,)), dma((n,)),
        ]
        + gather_sems,
        compiler_params=pltpu.CompilerParams(
            collective_id=0, has_side_effects=True, vmem_limit_bytes=58 * 1024 * 1024
        ),
    )(
        residual, norm_gain.reshape(width // 128, 128), frequency, lengths,
        query_weight, key_weight.T, value_weight.T, output_weight, past_cache,
    )
    entries = jnp.stack([keys[:, :, :robots], values[:, :, :robots]], axis=1)
    entries = entries.transpose(3, 0, 1, 2, 4).reshape(robots, STEPS, 2 * KVH * HD)
    return out, entries.astype(bf16)


def dispatch(*arrays):
    residual, _, query_weight, key_weight, _, _, past_cache, _ = arrays
    fits = (
        lax.axis_size("wide") == 16
        and residual.shape == (4, 8192)
        and query_weight.shape[1] == 512
        and key_weight.shape[1] == 64
        and past_cache.shape[1:] == (2, KVH, 512, HD)
    )
    return fused(*arrays) if fits else local(*arrays)


def solution(mesh):
    return jax.shard_map(
        dispatch,
        mesh=mesh,
        in_specs=(
            P(("groups", "wide"), None),
            P(),
            P(None, "wide"),
            P(None, "wide"),
            P(None, "wide"),
            P(None, "wide"),
            P(("groups", "wide"), None, None, None, None),
            P(("groups", "wide")),
        ),
        out_specs=(P(("groups", "wide"), None), P(("groups", "wide"), None, None)),
        check_vma=False,
    )
```

```python
import math
from functools import partial

import jax
import jax.numpy as jnp
import numpy as np
from jax import lax
from jax.experimental import pallas as pl
from jax.experimental.pallas import tpu as pltpu
from jax.sharding import PartitionSpec as P

QH = 64
KVH = 8
HD = 128
STEPS = 2


rope_base = 500000.0
norm_eps = 1e-05


def rotate_heads(heads_block, positions):
    head_size = heads_block.shape[-1]
    half_size = head_size // 2
    frequency = rope_base ** (-2.0 * jnp.arange(half_size, dtype=jnp.float32) / head_size)
    angles = positions.astype(jnp.float32)[:, None, None] * frequency[None, None, :]
    cosine = jnp.cos(angles)
    sine_part = jnp.sin(angles)
    values = heads_block.astype(jnp.float32)
    first_half = values[..., :half_size]
    second = values[..., half_size:]
    return jnp.concatenate(
        [first_half * cosine - second * sine_part, second * cosine + first_half * sine_part],
        axis=-1,
    ).astype(jnp.bfloat16)


def attend_local(queries, past_cache, fresh_keys, fresh_values, lengths, step_now):
    robots_here, head_count, head_size = queries.shape
    kv_heads = past_cache.shape[2]
    grouped = queries.reshape(robots_here, kv_heads, head_count // kv_heads, head_size)
    score_scale = 1.0 / math.sqrt(head_size)
    past_scores = (
        jnp.einsum("rkgd,rkcd->rkgc", grouped, past_cache[:, 0], preferred_element_type=jnp.float32)
        * score_scale
    )
    fresh_scores = (
        jnp.einsum("rkgd,rskd->rkgs", grouped, fresh_keys, preferred_element_type=jnp.float32)
        * score_scale
    )
    slot_index = jnp.arange(past_cache.shape[3], dtype=jnp.int32)
    past_scores = jnp.where(
        slot_index[None, None, None, :] < lengths[:, None, None, None], past_scores, -jnp.inf
    )
    turn_index = jnp.arange(fresh_keys.shape[1], dtype=jnp.int32)
    fresh_scores = jnp.where(turn_index[None, None, None, :] <= step_now, fresh_scores, -jnp.inf)
    peak_score = jnp.maximum(jnp.max(past_scores, axis=-1), jnp.max(fresh_scores, axis=-1))
    past_exp = jnp.exp(past_scores - peak_score[..., None])
    fresh_exp = jnp.exp(fresh_scores - peak_score[..., None])
    denominator = jnp.sum(past_exp, axis=-1) + jnp.sum(fresh_exp, axis=-1)
    past_weights = (past_exp / denominator[..., None]).astype(jnp.bfloat16)
    fresh_weights = (fresh_exp / denominator[..., None]).astype(jnp.bfloat16)
    context = jnp.einsum(
        "rkgc,rkcd->rkgd", past_weights, past_cache[:, 1], preferred_element_type=jnp.float32
    )
    context = context + jnp.einsum(
        "rkgs,rskd->rkgd", fresh_weights, fresh_values, preferred_element_type=jnp.float32
    )
    return context.reshape(robots_here, head_count * head_size).astype(jnp.bfloat16)


def local(
    residual, norm_gain, query_weight, key_weight, value_weight, output_weight, past_cache, lengths
):
    group_size = lax.axis_size("wide")
    robots_here, width = residual.shape
    query_cols = query_weight.shape[1]
    kv_cols = key_weight.shape[1]
    fresh_keys = jnp.zeros((robots_here, STEPS, KVH, HD), jnp.bfloat16)
    fresh_values = jnp.zeros((robots_here, STEPS, KVH, HD), jnp.bfloat16)
    final_state = residual
    for step_now in range(STEPS):
        widened = final_state.astype(jnp.float32)
        inverse_rms = lax.rsqrt(jnp.sum(widened * widened, axis=1) / width + norm_eps)
        normed = (widened * inverse_rms[:, None] * norm_gain[None, :]).astype(jnp.bfloat16)
        project_segment = lax.all_gather(normed, "wide", axis=0, tiled=True)
        projected = jnp.concatenate(
            [
                jnp.dot(project_segment, query_weight, preferred_element_type=jnp.float32),
                jnp.dot(project_segment, key_weight, preferred_element_type=jnp.float32),
                jnp.dot(project_segment, value_weight, preferred_element_type=jnp.float32),
            ],
            axis=1,
        ).astype(jnp.bfloat16)
        attend_fresh_keys = fresh_keys
        attend_fresh_values = fresh_values
        arrived = lax.all_to_all(projected, "wide", split_axis=0, concat_axis=1, tiled=True)
        blocks = arrived.reshape(robots_here, group_size, query_cols + 2 * kv_cols)
        positions = lengths + step_now
        queries = rotate_heads(blocks[:, :, :query_cols].reshape(robots_here, QH, HD), positions)
        new_keys = rotate_heads(
            blocks[:, :, query_cols : query_cols + kv_cols].reshape(robots_here, KVH, HD), positions
        )
        new_values = blocks[:, :, query_cols + kv_cols :].reshape(robots_here, KVH, HD)
        attend_fresh_keys = attend_fresh_keys.at[:, step_now].set(new_keys)
        attend_fresh_values = attend_fresh_values.at[:, step_now].set(new_values)
        context = attend_local(
            queries, past_cache, attend_fresh_keys, attend_fresh_values, lengths, step_now
        )
        attended = jnp.dot(
            lax.all_gather(context, "wide", axis=0, tiled=True),
            output_weight,
            preferred_element_type=jnp.float32,
        ).astype(jnp.bfloat16)
        attended, fresh_keys, fresh_values = (attended, attend_fresh_keys, attend_fresh_values)
        returned = lax.all_to_all(attended, "wide", split_axis=0, concat_axis=1, tiled=True)
        final_state = (final_state.astype(jnp.float32) + returned.astype(jnp.float32)).astype(
            jnp.bfloat16
        )
    new_entries = jnp.concatenate(
        [
            fresh_keys.reshape(robots_here, STEPS, KVH * HD),
            fresh_values.reshape(robots_here, STEPS, KVH * HD),
        ],
        axis=2,
    )
    return (final_state, new_entries)


def copy_to(src, dst, send_sem, recv_sem, peer):
    return pltpu.make_async_remote_copy(
        src_ref=src,
        dst_ref=dst,
        send_sem=send_sem,
        recv_sem=recv_sem,
        device_id={"wide": peer},
        device_id_type=pl.DeviceIdType.MESH,
    )


def exchange_start(n, me, src, dst, send, recv):
    def go(o, _):
        peer = lax.rem(me + o, n)
        copy_to(src.at[peer], dst.at[me], send.at[o], recv.at[o], peer).start()
        return 0

    lax.fori_loop(1, n, go, 0, unroll=True)
    dst[me] = src[me]


def exchange_finish(n, me, src, dst, send, recv):
    def go(o, _):
        peer = lax.rem(me + o, n)
        copy = copy_to(src.at[peer], dst.at[lax.rem(me + n - o, n)], send.at[o], recv.at[o], peer)
        copy.wait_recv()
        copy.wait_send()
        return 0

    lax.fori_loop(1, n, go, 0, unroll=True)


PIECES = 4
LAG = 2


class Gather:
    def __init__(self, n, me, buf, sems, pieces):
        self.n, self.me, self.buf = n, me, buf
        self.send, self.recv, self.pair_send, self.pair_recv = sems
        self.chips = n // 2
        self.rows = buf.shape[1] // pieces
        self.order = sorted(range(1, self.chips), key=lambda o: min(o, self.chips - o))

    def part(self, slot, c):
        return self.buf.at[slot, pl.ds(pl.multiple_of(c * self.rows, self.rows), self.rows)]

    def far(self, o, c):
        part = self.part(self.me, c)
        peer = lax.rem(self.me + 2 * o, self.n)
        return copy_to(part, part, self.send.at[c, o], self.recv.at[c, o], peer)

    def near(self, o, c):
        part = self.part(lax.rem(self.me + self.n - 2 * o, self.n), c)
        sibling = self.me + 1 - 2 * lax.rem(self.me, 2)
        return copy_to(part, part, self.pair_send.at[c, o], self.pair_recv.at[c, o], sibling)

    def start(self, c):
        for o in self.order[::-1]:
            self.far(o, c).start()
        self.near(0, c).start()

    def forward(self, c):
        for o in self.order:
            self.far(o, c).wait_recv()
            self.near(o, c).start()

    def arrive(self, c):
        for o in range(self.chips):
            self.near(o, c).wait_recv()

    def drain(self, c):
        self.near(0, c).wait_send()
        for o in self.order:
            self.far(o, c).wait_send()
            self.near(o, c).wait_send()


def layer_kernel(
    n,
    x0_ref, gain_ref, freq_ref, lengths_ref, wq_hbm, wk_hbm, wv_hbm, wo_hbm, cache_hbm,
    out_ref, keys_ref, values_ref,
    wq_ref, wkv_ref, wo_ref, cache_ref, xr_ref, xc_ref, xg_ref, pr_ref, m32_ref, sbuf_ref,
    rbuf_ref, cos_ref, sin_ref, rq_ref, cg_ref, t32_ref, acc_ref, fbuf_ref, fr_ref,
    load_sem, x_send, x_recv, q_send, q_recv, f_send, f_recv,
    *gather_sems,
):
    me = lax.axis_index("wide")
    robots = lengths_ref.shape[0]
    rows = n * robots
    width = wq_ref.shape[0]
    loads = [
        pltpu.make_async_copy(wk_hbm, wkv_ref.at[pl.ds(0, 64)], load_sem.at[0]),
        pltpu.make_async_copy(wv_hbm, wkv_ref.at[pl.ds(64, 64)], load_sem.at[1]),
        pltpu.make_async_copy(wq_hbm, wq_ref, load_sem.at[2]),
        pltpu.make_async_copy(cache_hbm, cache_ref, load_sem.at[3]),
        pltpu.make_async_copy(wo_hbm, wo_ref, load_sem.at[4]),
    ]
    for load in loads:
        load.start()
    barrier = pltpu.get_barrier_semaphore()

    def greet(o, _):
        pl.semaphore_signal(
            barrier, inc=1, device_id={"wide": lax.rem(me + o, n)}, device_id_type=pl.DeviceIdType.MESH
        )
        return 0

    lax.fori_loop(1, n, greet, 0)
    for k in range(4 * n):
        t32_ref[4 * k : 4 * k + 4] = x0_ref[:, 128 * k : 128 * k + 128].astype(jnp.float32)
    fbuf_ref[...] = t32_ref[0:256].reshape(n, 16, 128).astype(jnp.bfloat16)
    pl.semaphore_wait(barrier, n - 1)
    exchange_start(n, me, fbuf_ref, xr_ref, x_send, x_recv)

    robot_of = lax.broadcasted_iota(jnp.int32, (32, 128), 0) % robots
    lane = lax.broadcasted_iota(jnp.int32, (32, 128), 1)
    length = jnp.zeros((32, 128), jnp.int32)
    for r in range(robots):
        length = jnp.where(robot_of == r, lengths_ref[r], length)
    for t in range(STEPS):
        angles = (length + t).astype(jnp.float32) * freq_ref[...]
        cos_ref[t] = jnp.cos(angles)
        sine = jnp.sin(angles)
        sin_ref[t] = jnp.where(lane < HD // 2, -sine, sine)
    m32_ref[...] = jnp.zeros_like(m32_ref)
    keys_ref[...] = jnp.zeros_like(keys_ref)
    values_ref[...] = jnp.zeros_like(values_ref)

    exchange_finish(n, me, fbuf_ref, xr_ref, x_send, x_recv)
    t32_ref[0:256] = xr_ref[...].reshape(256, 128).astype(jnp.float32)
    for j in range(4):
        for r in range(robots):
            xc_ref[pl.ds(rows * j + r, n, stride=robots), :] = t32_ref[
                pl.ds(4 * j + r, n, stride=16), :
            ]
    for load in loads[:3]:
        load.wait()

    columns = Gather(n, me, xg_ref, gather_sems[:4], 1)
    contexts = Gather(n, me, cg_ref, gather_sems[4:], PIECES)

    def step(t, _):
        xg_ref[me] = xc_ref[...].astype(jnp.bfloat16)
        columns.start(0)
        columns.forward(0)
        columns.arrive(0)

        def square(s, total):
            x = xg_ref[s].astype(jnp.float32)
            x = x * x
            for j in range(4):
                total = total + x[rows * j : rows * j + rows]
            return total

        total = lax.fori_loop(0, n, square, jnp.zeros((rows, 128), jnp.float32), unroll=4)
        inverse = lax.rsqrt(jnp.sum(total, axis=1, keepdims=True) / width + norm_eps)
        inverse = jnp.broadcast_to(inverse, (rows, 128))
        acc_ref[...] = jnp.zeros_like(acc_ref)

        def project(s, _):
            parts = []
            for j in range(4):
                x = xg_ref[s, rows * j : rows * j + rows].astype(jnp.float32)
                parts.append((x * inverse * gain_ref[pl.ds(4 * s + j, 1), :]).astype(jnp.bfloat16))
            normed = jnp.concatenate(parts, axis=1)
            part = pl.ds(pl.multiple_of(s * 512, 512), 512)
            acc_ref[:, 0:512] += jnp.dot(
                normed, wq_ref[part, :], preferred_element_type=jnp.float32
            )
            acc_ref[:, 512:640] += lax.dot_general(
                normed,
                wkv_ref[:, part],
                (((1,), (1,)), ((), ())),
                preferred_element_type=jnp.float32,
            )
            return 0

        lax.fori_loop(0, n, project, 0, unroll=4)
        for j in range(5):
            pr_ref[rows * j : rows * j + rows] = acc_ref[:, 128 * j : 128 * j + 128]
        for j in range(5):
            for r in range(robots):
                m32_ref[pl.ds(4 * j + r, n, stride=32), :] = pr_ref[
                    pl.ds(rows * j + r, n, stride=robots), :
                ]
        sbuf_ref[...] = m32_ref[...].reshape(n, 32, 128).astype(jnp.bfloat16)
        exchange_start(n, me, sbuf_ref, rbuf_ref, q_send, q_recv)

        @pl.when(t == 0)
        def _():
            loads[3].wait()

        columns.drain(0)
        exchange_finish(n, me, sbuf_ref, rbuf_ref, q_send, q_recv)
        cosine = cos_ref[t]
        sine = sin_ref[t]
        slot = lax.broadcasted_iota(jnp.int32, (8, 512), 1)
        low = lax.broadcasted_iota(jnp.int32, (8, 128), 1) < HD // 2
        scale = 1.0 / math.sqrt(HD)

        def attend(g, _):
            first = rbuf_ref[2 * g].astype(jnp.float32)
            second = rbuf_ref[2 * g + 1].astype(jnp.float32)
            q = jnp.concatenate([first[:16], second[:16]], axis=0)
            q = q * cosine + pltpu.roll(q, HD // 2, 1) * sine
            rq_ref[...] = q.astype(jnp.bfloat16).astype(jnp.float32)
            a, b = first[16:24], second[16:24]
            k = jnp.where(low, a, pltpu.roll(b, HD // 2, 1))
            v = jnp.where(low, pltpu.roll(a, HD // 2, 1), b)
            k = k * cosine[:8] + pltpu.roll(k, HD // 2, 1) * sine[:8]
            keys_ref[t, g] = k.astype(jnp.bfloat16).astype(jnp.float32)
            values_ref[t, g] = v
            past, fresh = [], []
            for r in range(robots):
                q = rq_ref[pl.ds(r, 8, stride=robots), :]
                s = lax.dot_general(
                    q.astype(jnp.bfloat16),
                    cache_ref[r, 0, g],
                    (((1,), (1,)), ((), ())),
                    preferred_element_type=jnp.float32,
                )
                past.append(jnp.where(slot < lengths_ref[r], s * scale, -jnp.inf))
                fresh.append(
                    [
                        jnp.sum(q * keys_ref[i, g, r : r + 1, :], axis=1, keepdims=True) * scale
                        for i in range(STEPS)
                    ]
                )
            past = jnp.concatenate(past, axis=0)
            fresh = [jnp.concatenate([f[i] for f in fresh], axis=0) for i in range(STEPS)]
            for i in range(1, STEPS):
                fresh[i] = jnp.where(i <= t, fresh[i], -jnp.inf)
            peak = jnp.max(past, axis=1, keepdims=True)
            for f in fresh:
                peak = jnp.maximum(peak, f)
            past = jnp.exp(past - peak)
            fresh = [jnp.exp(f - peak) for f in fresh]
            denominator = jnp.sum(past, axis=1, keepdims=True)
            for f in fresh:
                denominator = denominator + f
            past = past / denominator
            fresh = [(f / denominator).astype(jnp.bfloat16).astype(jnp.float32) for f in fresh]
            context = []
            for r in range(robots):
                c = jnp.dot(
                    past[8 * r : 8 * r + 8].astype(jnp.bfloat16),
                    cache_ref[r, 1, g],
                    preferred_element_type=jnp.float32,
                )
                for i in range(STEPS):
                    c = c + fresh[i][8 * r : 8 * r + 8] * values_ref[i, g, r : r + 1, :]
                context.append(c)
            cg_ref[me, pl.ds(pl.multiple_of(g * 32, 32), 32), :] = jnp.concatenate(
                context, axis=0
            ).astype(jnp.bfloat16)
            return 0

        each = KVH // PIECES

        def attend_piece(c, _):
            [attend(c * each + i, 0) for i in range(each)]
            contexts.start(c)

            @pl.when(c >= LAG)
            def _():
                contexts.forward(c - LAG)

            return 0

        lax.fori_loop(0, PIECES, attend_piece, 0)

        @pl.when(t == 0)
        def _():
            loads[4].wait()

        acc_ref[...] = jnp.zeros_like(acc_ref)

        def output(g, _):
            block = cg_ref[:, pl.ds(pl.multiple_of(g * 32, 32), 32), :]
            t32_ref[...] = block.reshape(n * 32, 128).astype(jnp.float32)
            left = jnp.concatenate(
                [t32_ref[pl.ds(h, rows, stride=8), :].astype(jnp.bfloat16) for h in range(8)], axis=1
            )
            acc_ref[:, 0:512] += jnp.dot(
                left,
                wo_ref[pl.ds(pl.multiple_of(g * 1024, 1024), 1024), :],
                preferred_element_type=jnp.float32,
            )
            return 0

        def output_piece(c, _):
            @pl.when(c + PIECES - LAG < PIECES)
            def _():
                contexts.forward(c + PIECES - LAG)

            contexts.arrive(c)
            [output(c * each + i, 0) for i in range(each)]
            return 0

        lax.fori_loop(0, PIECES, output_piece, 0)
        for j in range(4):
            part = slice(rows * j, rows * j + rows)
            attended = acc_ref[:, 128 * j : 128 * j + 128].astype(jnp.bfloat16).astype(jnp.float32)
            xc_ref[part] = (xc_ref[part] + attended).astype(jnp.bfloat16).astype(jnp.float32)

        def drain(c, _):
            contexts.drain(c)
            return 0

        lax.fori_loop(0, PIECES, drain, 0)
        return 0

    lax.fori_loop(0, STEPS, step, 0)
    for j in range(4):
        for r in range(robots):
            t32_ref[pl.ds(4 * j + r, n, stride=16), :] = xc_ref[
                pl.ds(rows * j + r, n, stride=robots), :
            ]
    fbuf_ref[...] = t32_ref[0:256].reshape(n, 16, 128).astype(jnp.bfloat16)
    exchange_start(n, me, fbuf_ref, fr_ref, f_send, f_recv)
    exchange_finish(n, me, fbuf_ref, fr_ref, f_send, f_recv)
    t32_ref[0:256] = fr_ref[...].reshape(256, 128).astype(jnp.float32)
    for k in range(4 * n):
        out_ref[:, 128 * k : 128 * k + 128] = t32_ref[4 * k : 4 * k + 4].astype(jnp.bfloat16)


def fused(
    residual, norm_gain, query_weight, key_weight, value_weight, output_weight, past_cache, lengths
):
    n = lax.axis_size("wide")
    robots, width = residual.shape
    frequency = np.tile(rope_base ** (-2.0 * np.arange(HD // 2) / HD), 2)
    frequency = jnp.asarray(frequency[None, :], jnp.float32)
    vmem = pl.BlockSpec(memory_space=pltpu.VMEM)
    smem = pl.BlockSpec(memory_space=pltpu.SMEM)
    any_spec = pl.BlockSpec(memory_space=pl.ANY)
    bf16, f32 = jnp.bfloat16, jnp.float32
    dma = pltpu.SemaphoreType.DMA
    gather_sems = [dma((1, n // 2))] * 4 + [dma((PIECES, n // 2))] * 4
    out, keys, values = pl.pallas_call(
        partial(layer_kernel, n),
        out_shape=(
            jax.ShapeDtypeStruct((robots, width), bf16),
            jax.ShapeDtypeStruct((STEPS, KVH, 8, HD), f32),
            jax.ShapeDtypeStruct((STEPS, KVH, 8, HD), f32),
        ),
        in_specs=[vmem, vmem, vmem, smem] + [any_spec] * 5,
        out_specs=(vmem, vmem, vmem),
        scratch_shapes=[
            pltpu.VMEM(query_weight.shape, bf16),
            pltpu.VMEM((2 * key_weight.shape[1], width), bf16),
            pltpu.VMEM(output_weight.shape, bf16),
            pltpu.VMEM(past_cache.shape, bf16),
            pltpu.VMEM((n, 16, 128), bf16),
            pltpu.VMEM((n * 16, 128), f32),
            pltpu.VMEM((n, n * 16, 128), bf16),
            pltpu.VMEM((5 * n * robots, 128), f32),
            pltpu.VMEM((n * 32, 128), f32),
            pltpu.VMEM((n, 32, 128), bf16),
            pltpu.VMEM((n, 32, 128), bf16),
            pltpu.VMEM((STEPS, 32, 128), f32),
            pltpu.VMEM((STEPS, 32, 128), f32),
            pltpu.VMEM((32, 128), f32),
            pltpu.VMEM((n, KVH * 32, 128), bf16),
            pltpu.VMEM((n * 32, 128), f32),
            pltpu.VMEM((n * robots, 640), f32),
            pltpu.VMEM((n, 16, 128), bf16),
            pltpu.VMEM((n, 16, 128), bf16),
            dma((5,)),
            dma((n,)), dma((n,)), dma((n,)), dma((n,)), dma((n,)), dma((n,)),
        ]
        + gather_sems,
        compiler_params=pltpu.CompilerParams(
            collective_id=0, has_side_effects=True, vmem_limit_bytes=58 * 1024 * 1024
        ),
    )(
        residual, norm_gain.reshape(width // 128, 128), frequency, lengths,
        query_weight, key_weight.T, value_weight.T, output_weight, past_cache,
    )
    entries = jnp.stack([keys[:, :, :robots], values[:, :, :robots]], axis=1)
    entries = entries.transpose(3, 0, 1, 2, 4).reshape(robots, STEPS, 2 * KVH * HD)
    return out, entries.astype(bf16)


def dispatch(*arrays):
    residual, _, query_weight, key_weight, _, _, past_cache, _ = arrays
    fits = (
        lax.axis_size("wide") == 16
        and residual.shape == (4, 8192)
        and query_weight.shape[1] == 512
        and key_weight.shape[1] == 64
        and past_cache.shape[1:] == (2, KVH, 512, HD)
    )
    return fused(*arrays) if fits else local(*arrays)


def solution(mesh):
    return jax.shard_map(
        dispatch,
        mesh=mesh,
        in_specs=(
            P(("groups", "wide"), None),
            P(),
            P(None, "wide"),
            P(None, "wide"),
            P(None, "wide"),
            P(None, "wide"),
            P(("groups", "wide"), None, None, None, None),
            P(("groups", "wide")),
        ),
        out_specs=(P(("groups", "wide"), None), P(("groups", "wide"), None, None)),
        check_vma=False,
    )
```
